32 devices in a mesh: seq: 8 (over y, x, core), tp: 4 (over z).
Axes of the slice: x: 2, y: 2, z: 4, core: 2. Of those that a mesh axis runs over, the one named last changes fastest.
Arguments:
- queries: bfloat16 [2048, 4096], P('seq', 'tp'), may hold values from -5 to 5
- keys: bfloat16 [2048, 1024], P('seq'), may hold values from -5 to 5
- values: bfloat16 [2048, 1024], P('seq'), may hold values from -6 to 6
- out_weight: bfloat16 [4096, 5120], P('tp'), may hold values from -0.29882812 to 0.29882812
Outputs:
- projected: bfloat16 [2048, 5120], P(('seq', 'tp'))
The draws below stay inside these ranges and needn't reach their ends.
All inputs are finite; a program needn't handle non-finite values.
Results may differ from the reference program's by a relative error of at most 0.012.
Values may be sent and summed in bfloat16 or wider, within the bound.
No kernel may reach another device: no remote copies, remote signals or barrier semaphores. Data moves between devices by JAX's collectives and lax.ppermute only.
A program may use at most 64 MiB of HBM per device.

```python
import jax
import jax.numpy as jnp
from jax import lax

D = 5120
QUERY_HEADS = 32
KEY_VALUE_HEADS = 8
HEAD_DIMENSION = 128
STRETCH = 8192
TOK_DEV = 256
SEQUENCE_TOKENS = 2048
N_SEQ = 8
N_TP = 4


def draw_keys(key, part):
    layer_result = jnp.clip(jax.random.normal(jax.random.fold_in(key, 1), (SEQUENCE_TOKENS, KEY_VALUE_HEADS * HEAD_DIMENSION), jnp.float32), -4.5, 4.5)
    return layer_result.astype(jnp.bfloat16)


def draw_queries(key, part):
    layer_result = jnp.clip(jax.random.normal(jax.random.fold_in(key, 2), (SEQUENCE_TOKENS, QUERY_HEADS * HEAD_DIMENSION), jnp.float32), -4.5, 4.5)
    return layer_result.astype(jnp.bfloat16)


def block_levels(key, dims, split, low, high):
    gain, own = 1.0, jax.random.fold_in(key, 6)
    for dim, blocks in split:
        heights = jnp.exp(jax.random.uniform(jax.random.fold_in(own, dim), (blocks,), jnp.float32, low / len(split), high / len(split)))
        gain = gain * jnp.repeat(heights, dims[dim] // blocks).reshape([-1 if axis == dim else 1 for axis in range(len(dims))])
    return gain


def centred(rng, extent, spread, limit, shards=(), kind=jnp.bfloat16):
    gain = block_levels(rng, extent, shards, -0.22, 0.18) if shards else 1.0
    entries = jax.random.normal(rng, extent, jnp.float32) * spread * gain
    return jnp.minimum(jnp.maximum(entries, -limit), limit).astype(kind)


def setup_inputs(seed: int = 0) -> dict:
    key_list = jax.random.split(jax.random.key(seed), 5)
    return {
        "queries": draw_queries(jax.random.fold_in(key_list[4], 71), 0),
        "keys": draw_keys(jax.random.fold_in(key_list[4], 71), 0),
        "values": centred(key_list[2], (SEQUENCE_TOKENS, KEY_VALUE_HEADS * HEAD_DIMENSION), 1.0, 6.0, ((0, 8),)),
        "out_weight": centred(key_list[3], (QUERY_HEADS * HEAD_DIMENSION, D), 0.05, 0.29882812, ((0, 4),)),
    }


def reference(queries, keys, values, out_weight):
    query_group = QUERY_HEADS // KEY_VALUE_HEADS
    stretch_amount = TOK_DEV * min(STRETCH // TOK_DEV, N_SEQ)
    token_count = SEQUENCE_TOKENS // stretch_amount
    scale = HEAD_DIMENSION ** -0.5
    q_all = queries.reshape(token_count, stretch_amount, QUERY_HEADS, HEAD_DIMENSION)
    all_keys = keys.reshape(token_count, stretch_amount, KEY_VALUE_HEADS, HEAD_DIMENSION)
    all_values = values.reshape(token_count, stretch_amount, KEY_VALUE_HEADS, HEAD_DIMENSION)
    place = jnp.arange(stretch_amount)
    causal = place[None, :] <= place[:, None]

    def one_head(head):
        kv_head = head // query_group

        def one_block(block):
            q_rows = q_all[block, :, head]
            k_rows = all_keys[block, :, kv_head]
            v_rows = all_values[block, :, kv_head]
            score = jnp.dot(q_rows, k_rows.T, preferred_element_type=jnp.float32) * scale
            score = jnp.where(causal, score, -1e30)
            top = jnp.max(score, axis=1, keepdims=True)
            weight = jnp.exp(score - top)
            total = jnp.sum(weight, axis=1, keepdims=True)
            mixed = jnp.dot(weight.astype(jnp.bfloat16), v_rows, preferred_element_type=jnp.float32)
            return (mixed / total).astype(jnp.bfloat16)

        return lax.map(one_block, jnp.arange(token_count))

    heads = lax.map(one_head, jnp.arange(QUERY_HEADS))
    attended = jnp.transpose(heads, (1, 2, 0, 3)).reshape(SEQUENCE_TOKENS, QUERY_HEADS * HEAD_DIMENSION)
    width = QUERY_HEADS * HEAD_DIMENSION // N_TP
    summed = jnp.zeros((SEQUENCE_TOKENS, D), jnp.float32)
    for group_index in range(N_TP):
        part_cols = attended[:, group_index * width:(group_index + 1) * width]
        part_rows = out_weight[group_index * width:(group_index + 1) * width]
        partial_sum = jnp.dot(part_cols, part_rows, preferred_element_type=jnp.float32)
        summed = summed + partial_sum.astype(jnp.bfloat16).astype(jnp.float32)
    return summed.astype(jnp.bfloat16)
```

```python
import functools
import math

import jax
import jax.numpy as jnp
from jax import lax
from jax.experimental import pallas as pl
from jax.experimental.pallas import tpu as pltpu
from jax.sharding import PartitionSpec as P

QUERY_HEADS = 32
KEY_VALUE_HEADS = 8
HEAD_DIMENSION = 128
STRETCH = 8192
LANES = 128
EXPONENT = HEAD_DIMENSION ** (-0.5) * math.log2(math.e)
NEGATIVE = -1e30
VMEM_LIMIT = 48 * 1024 * 1024


def dot_nt(a, b):
    return lax.dot_general(a, b, (((1,), (1,)), ((), ())), preferred_element_type=jnp.float32)


def spread(column):
    return jnp.broadcast_to(column, (column.shape[0], LANES))


def fold(q_ref, pairs, acc_ref, top_ref, total_ref, heads, per_kv):
    hd = HEAD_DIMENSION
    kv_here = heads // per_kv
    for h in range(heads):
        g = h // per_kv
        q = q_ref[:, h * hd : (h + 1) * hd]
        score = jnp.concatenate(
            [dot_nt(q, pair[:, g * hd : (g + 1) * hd]) for pair in pairs], axis=1
        )
        score = score * EXPONENT
        old = top_ref[h]
        new = jnp.maximum(old, spread(jnp.max(score, axis=1, keepdims=True)))
        shrink = jnp.exp2(old - new)
        weight = jnp.exp2(score - new[:, :1])
        total_ref[h] = total_ref[h] * shrink + spread(jnp.sum(weight, axis=1, keepdims=True))
        weight = weight.astype(jnp.bfloat16)
        mixed = None
        at = 0
        for pair in pairs:
            rows = pair.shape[0]
            part = jnp.dot(
                weight[:, at : at + rows],
                pair[:, (kv_here + g) * hd : (kv_here + g + 1) * hd],
                preferred_element_type=jnp.float32,
            )
            mixed = part if mixed is None else mixed + part
            at += rows
        acc_ref[h] = acc_ref[h] * shrink + mixed
        top_ref[h] = new


def own_kernel(flags, q_ref, own_ref, other_ref, acc_ref, top_ref, total_ref, *, heads, per_kv):
    hd = HEAD_DIMENSION
    kv_here = heads // per_kv
    tok = q_ref.shape[0]
    visible = lax.broadcasted_iota(jnp.int32, (tok, tok), 0) >= lax.broadcasted_iota(
        jnp.int32, (tok, tok), 1
    )
    for h in range(heads):
        g = h // per_kv
        score = dot_nt(q_ref[:, h * hd : (h + 1) * hd], own_ref[:, g * hd : (g + 1) * hd])
        score = jnp.where(visible, score * EXPONENT, NEGATIVE)
        top = jnp.max(score, axis=1, keepdims=True)
        weight = jnp.exp2(score - top)
        top_ref[h] = spread(top)
        total_ref[h] = spread(jnp.sum(weight, axis=1, keepdims=True))
        acc_ref[h] = jnp.dot(
            weight.astype(jnp.bfloat16),
            own_ref[:, (kv_here + g) * hd : (kv_here + g + 1) * hd],
            preferred_element_type=jnp.float32,
        )

    @pl.when(flags[0] > 0)
    def _():
        fold(q_ref, [other_ref], acc_ref, top_ref, total_ref, heads, per_kv)


def rest_kernel(flags, q_ref, acc_in, top_in, total_in, *refs, heads, per_kv, chips, chunks, tile):
    hd = HEAD_DIMENSION
    blocks, refs = refs[: 2 * chips], refs[2 * chips :]
    w_hbm, refs = refs[0], refs[1:]
    outs, refs = refs[:chunks], refs[chunks:]
    acc_ref, top_ref, total_ref, att_ref, w_ref, sems = refs
    tiles = w_hbm.shape[1] // tile
    copies = [
        pltpu.make_async_copy(
            w_hbm.at[:, pl.ds(i * tile, tile)], w_ref.at[:, pl.ds(i * tile, tile)], sems.at[i]
        )
        for i in range(tiles)
    ]
    for copy in copies:
        copy.start()
    acc_ref[...] = acc_in[...]
    top_ref[...] = top_in[...]
    total_ref[...] = total_in[...]
    for d in range(chips):

        @pl.when(flags[d] > 0)
        def _(d=d):
            pair = [blocks[2 * d], blocks[2 * d + 1]]
            fold(q_ref, pair, acc_ref, top_ref, total_ref, heads, per_kv)

    for h in range(heads):
        att_ref[:, h * hd : (h + 1) * hd] = (acc_ref[h] / total_ref[h]).astype(jnp.bfloat16)
    rows = q_ref.shape[0] // chunks
    order = [
        att_ref[pl.ds(pl.multiple_of(flags[chips + i] * rows, rows), rows), :]
        for i in range(chunks)
    ]
    attended = jnp.concatenate(order, axis=0)
    for i in range(tiles):
        copies[i].wait()
        cols = slice(i * tile, (i + 1) * tile)
        part = jnp.dot(attended, w_ref[:, cols], preferred_element_type=jnp.float32)
        for j in range(chunks):
            outs[j][:, cols] = part[j * rows : (j + 1) * rows].astype(jnp.bfloat16)


def whole_block(shape):
    return pl.BlockSpec(shape, lambda *_: (0,) * len(shape))


def added(*terms):
    total = terms[0].astype(jnp.float32)
    for term in terms[1:]:
        total = total + term.astype(jnp.float32)
    return total.astype(terms[0].dtype)


def body(queries, keys, values, out_weight):
    tok = queries.shape[0]
    hd = HEAD_DIMENSION
    heads = queries.shape[1] // hd
    group = QUERY_HEADS // KEY_VALUE_HEADS
    kv_here = max(1, heads // group)
    per_kv = heads // kv_here
    width = out_weight.shape[1]
    seq_devs, tp_devs = lax.axis_size("seq"), lax.axis_size("tp")
    seq_at, tp_at = lax.axis_index("seq"), lax.axis_index("tp")
    first = tp_at * heads // group * hd
    own = jnp.concatenate(
        [lax.dynamic_slice_in_dim(x, first, kv_here * hd, 1) for x in (keys, values)], axis=1
    )
    devs = min(STRETCH // tok, seq_devs)
    chips = devs // 2
    place = seq_at % devs
    chip, core = place // 2, place % 2

    swap = [(i, i ^ 1) for i in range(seq_devs)]
    blocks, valid = [], []
    for d in range(chips - 1, 0, -1):
        pairs = [(i, i ^ (2 * d)) for i in range(seq_devs) if i ^ (2 * d) > i]
        blocks.append(lax.ppermute(own, "seq", pairs))
        valid.append(((chip ^ d) < chip).astype(jnp.int32))
    other = lax.ppermute(own, "seq", swap)
    both = []
    for block in blocks:
        both += [block, lax.ppermute(block, "seq", swap)]

    state = [jax.ShapeDtypeStruct((heads, tok, LANES), jnp.float32)] * 3
    state_block = whole_block((heads, tok, LANES))
    pair_block = whole_block(own.shape)
    q_block = whole_block(queries.shape)
    acc, top, total = pl.pallas_call(
        functools.partial(own_kernel, heads=heads, per_kv=per_kv),
        grid_spec=pltpu.PrefetchScalarGridSpec(
            num_scalar_prefetch=1,
            grid=(1,),
            in_specs=[q_block, pair_block, pair_block],
            out_specs=[state_block] * 3,
        ),
        out_shape=state,
        compiler_params=pltpu.CompilerParams(vmem_limit_bytes=VMEM_LIMIT),
        cost_estimate=pl.CostEstimate(
            flops=8 * heads * tok * tok * hd, bytes_accessed=4 * 2**20, transcendentals=0
        ),
    )(core[None].astype(jnp.int32), queries, own, other)

    chunks = tp_devs if tp_devs == 4 else 1
    if chunks == 4:
        low = tp_at < 2
        order = [
            jnp.where(low, 3, 0),
            jnp.where(low, 2, 1),
            tp_at ^ 1,
            tp_at,
        ]
    else:
        order = [jnp.int32(0)]
    flags = jnp.stack(valid + [o.astype(jnp.int32) for o in order])
    rows = tok // chunks
    tile = 512
    parts = pl.pallas_call(
        functools.partial(
            rest_kernel, heads=heads, per_kv=per_kv, chips=chips - 1, chunks=chunks, tile=tile
        ),
        grid_spec=pltpu.PrefetchScalarGridSpec(
            num_scalar_prefetch=1,
            grid=(1,),
            in_specs=[q_block]
            + [state_block] * 3
            + [pair_block] * len(both)
            + [pl.BlockSpec(memory_space=pl.ANY)],
            out_specs=[whole_block((rows, width))] * chunks,
            scratch_shapes=[pltpu.VMEM((heads, tok, LANES), jnp.float32)] * 3
            + [
                pltpu.VMEM((tok, heads * hd), jnp.bfloat16),
                pltpu.VMEM(out_weight.shape, jnp.bfloat16),
                pltpu.SemaphoreType.DMA((width // tile,)),
            ],
        ),
        out_shape=[jax.ShapeDtypeStruct((rows, width), jnp.bfloat16)] * chunks,
        compiler_params=pltpu.CompilerParams(vmem_limit_bytes=VMEM_LIMIT),
        cost_estimate=pl.CostEstimate(
            flops=2 * tok * width * heads * hd, bytes_accessed=16 * 2**20, transcendentals=0
        ),
    )(flags, queries, acc, top, total, *both, out_weight)

    if chunks == 1:
        return lax.psum_scatter(parts[0], "tp", scatter_dimension=0, tiled=True)
    far, near, side, mine = parts
    inward, sides = [(0, 1), (3, 2)], [(0, 1), (1, 0), (2, 3), (3, 2)]
    half = rows // 2
    got_far = lax.ppermute(far, "tp", inward)
    got_near = [lax.ppermute(x, "tp", inward) for x in (near[:half], near[half:])]
    got_side = lax.ppermute(side, "tp", sides)
    across_far = lax.ppermute(added(got_far, far), "tp", [(1, 3), (2, 0)])
    across_near = [
        lax.ppermute(added(got, x), "tp", [(1, 2), (2, 1)])
        for got, x in zip(got_near, (near[:half], near[half:]))
    ]
    return added(mine, got_side, across_far, jnp.concatenate(across_near, axis=0))


def solution(mesh):
    return jax.shard_map(
        body,
        mesh=mesh,
        in_specs=(P("seq", "tp"), P("seq", None), P("seq", None), P("tp", None)),
        out_specs=P(("seq", "tp"), None),
        check_vma=False,
    )
```

```python
import functools
import math

import jax
import jax.numpy as jnp
from jax import lax
from jax.experimental import pallas as pl
from jax.experimental.pallas import tpu as pltpu
from jax.sharding import PartitionSpec as P

QUERY_HEADS = 32
KEY_VALUE_HEADS = 8
HEAD_DIMENSION = 128
STRETCH = 8192
EXPONENT = HEAD_DIMENSION ** (-0.5) * math.log2(math.e)
NEGATIVE = -1e30
TILE = 512


def dot(a, b):
    return jnp.dot(a, b, preferred_element_type=jnp.float32)


def dot_nt(a, b):
    return lax.dot_general(a, b, (((1,), (1,)), ((), ())), preferred_element_type=jnp.float32)


def head(index):
    return slice(index * HEAD_DIMENSION, (index + 1) * HEAD_DIMENSION)


def spread(column):
    return jnp.broadcast_to(column, (column.shape[0], HEAD_DIMENSION))


def keys_of(first, second, g):
    return jnp.concatenate([first[:, head(g)], second[:, head(g)]], axis=0)


def values_of(first, second, g, kv_here):
    values = keys_of(first, second, kv_here + g)
    return jnp.concatenate([values, jnp.ones_like(values)], axis=1)


def folded(query, keys, values, acc, top):
    score = dot_nt(query, keys)
    new = jnp.maximum(top, spread(jnp.max(score, axis=1, keepdims=True)))
    shrink = jnp.exp2((top - new) * EXPONENT)
    weight = jnp.exp2((score - new[:, :1]) * EXPONENT).astype(jnp.bfloat16)
    return acc * jnp.concatenate([shrink, shrink], axis=1) + dot(weight, values), new


def fetch(pairs, sems):
    copies = [pltpu.make_async_copy(src, dst, sems.at[i]) for i, (src, dst) in enumerate(pairs)]
    for copy in copies:
        copy.start()
    return copies


def pack_kernel(keys, values, own_ref, sems, *, per_kv, heads):
    half = own_ref.shape[1] // 2
    at = lax.axis_index("tp")
    if heads < per_kv:
        at = lax.div(at, per_kv // heads)
    cols = pl.ds(pl.multiple_of(at * half, HEAD_DIMENSION), half)
    for copy in fetch(
        [(keys.at[:, cols], own_ref.at[:, :half]), (values.at[:, cols], own_ref.at[:, half:])], sems
    ):
        copy.wait()


def stage_kernel(*refs):
    half = (len(refs) - 1) // 2
    for copy in fetch(list(zip(refs[:half], refs[half : 2 * half])), refs[-1]):
        copy.wait()


def layer_kernel(q_ref, *refs, heads, per_kv, chips, order):
    chunks = len(order)
    kv_ref, refs = refs[: 2 * chips], refs[2 * chips :]
    w_ref, outs, refs = refs[0], refs[1 : 1 + chunks], refs[1 + chunks :]
    acc_ref, top_ref, att_ref = refs
    rows = outs[0].shape[0]
    tok = kv_ref[0].shape[0]
    kv_here = heads // per_kv
    place = lax.rem(lax.axis_index("seq"), 2 * chips)
    chip, core = lax.div(place, 2), lax.rem(place, 2)
    tp_at = lax.axis_index("tp")
    starts = [pl.multiple_of(chunk(tp_at) * rows, rows) for chunk in order]
    there = [pl.ds(start, rows) for start in starts]
    here = [slice(i * rows, (i + 1) * rows) for i in range(chunks)]

    def every(step):
        for i in range(chunks):
            for g in range(kv_here):
                mine = range(g * per_kv, (g + 1) * per_kv)
                step(i, g, jnp.concatenate([q_ref[there[i], head(h)] for h in mine], axis=0))

    def own(i, g, query):
        score = dot_nt(query, keys_of(kv_ref[0], kv_ref[1], g))
        row = lax.broadcasted_iota(jnp.int32, score.shape, 0) % rows + starts[i]
        col = lax.broadcasted_iota(jnp.int32, score.shape, 1)
        score = jnp.where(col <= jnp.where(col < tok, row, core * 2 * tok), score, NEGATIVE)
        top = jnp.max(score, axis=1, keepdims=True)
        weight = jnp.exp2((score - top) * EXPONENT).astype(jnp.bfloat16)
        acc_ref[i, g] = dot(weight, values_of(kv_ref[0], kv_ref[1], g, kv_here))
        top_ref[i, g] = spread(top)

    def others(i, g, query, pair=None):
        acc_ref[i, g], top_ref[i, g] = folded(
            query,
            keys_of(*pair, g),
            values_of(*pair, g, kv_here),
            acc_ref[i, g],
            top_ref[i, g],
        )

    for d in range(chips):
        if d == 0:
            every(own)
        else:
            pair = (kv_ref[2 * d], kv_ref[2 * d + 1])
            pl.when((chip ^ d) < chip)(
                functools.partial(every, functools.partial(others, pair=pair))
            )
    for i in range(chunks):
        for h in range(heads):
            g, j = h // per_kv, h % per_kv
            state = acc_ref[i, g, j * rows : (j + 1) * rows, :]
            att_ref[here[i], head(h)] = (
                state[:, :HEAD_DIMENSION] / state[:, HEAD_DIMENSION:]
            ).astype(jnp.bfloat16)
    attended = att_ref[...]
    for at in range(0, w_ref.shape[1], TILE):
        part = dot(attended, w_ref[:, at : at + TILE]).astype(jnp.bfloat16)
        for i in range(chunks):
            outs[i][:, at : at + TILE] = part[here[i]]


def call(kernel, out_shape, *args, scratch, limit, place=pltpu.VMEM):
    return pl.pallas_call(
        kernel,
        out_shape=out_shape,
        in_specs=[pl.BlockSpec(memory_space=place)] * len(args),
        out_specs=[pl.BlockSpec(memory_space=pltpu.VMEM)] * len(out_shape),
        scratch_shapes=scratch,
        compiler_params=pltpu.CompilerParams(vmem_limit_bytes=limit * 2**20),
    )(*args)


def after(value, *others):
    return lax.optimization_barrier((value, *others))[0]


def added(*terms):
    total = terms[0].astype(jnp.float32)
    for term in terms[1:]:
        total = total + term.astype(jnp.float32)
    return total.astype(terms[0].dtype)


def body(queries, keys, values, out_weight):
    tok = queries.shape[0]
    hd = HEAD_DIMENSION
    heads = queries.shape[1] // hd
    group = QUERY_HEADS // KEY_VALUE_HEADS
    kv_here = max(1, heads // group)
    per_kv = heads // kv_here
    width = out_weight.shape[1]
    seq_devs, tp_devs = lax.axis_size("seq"), lax.axis_size("tp")
    pair_shape = (tok, 2 * kv_here * hd)
    semaphores = pltpu.SemaphoreType.DMA
    (own,) = call(
        functools.partial(pack_kernel, per_kv=group, heads=heads),
        [jax.ShapeDtypeStruct(pair_shape, keys.dtype)],
        keys,
        values,
        scratch=[semaphores((2,))],
        limit=56,
        place=pl.ANY,
    )
    devs = min(STRETCH // tok, seq_devs)
    chips = devs // 2

    swap = [(i, i ^ 1) for i in range(seq_devs)]
    blocks = [own]
    for d in range(1, chips):
        pairs = [(i, i ^ (2 * d)) for i in range(seq_devs) if i ^ (2 * d) > i]
        blocks.append(lax.ppermute(own, "seq", pairs))
    q_here, w_here = call(
        stage_kernel,
        [jax.ShapeDtypeStruct(x.shape, x.dtype) for x in (queries, out_weight)],
        queries,
        out_weight,
        scratch=[semaphores((2,))],
        limit=24,
        place=pl.ANY,
    )
    blocks[1:] = lax.optimization_barrier((*blocks[1:], q_here, w_here))[: chips - 1]
    both = []
    for block in blocks:
        both += [block, lax.ppermute(block, "seq", swap)]

    def layer(order, rows):
        chunks = len(order)
        return call(
            functools.partial(layer_kernel, heads=heads, per_kv=per_kv, chips=chips, order=order),
            [jax.ShapeDtypeStruct((rows, width), jnp.bfloat16)] * chunks,
            q_here,
            *both,
            w_here,
            scratch=[
                pltpu.VMEM((chunks, kv_here, per_kv * rows, 2 * hd), jnp.float32),
                pltpu.VMEM((chunks, kv_here, per_kv * rows, hd), jnp.float32),
                pltpu.VMEM((rows * chunks, heads * hd), jnp.bfloat16),
            ],
            limit=24,
        )

    if tp_devs != 4:
        (part,) = layer([lambda at: 0], tok)
        return lax.psum_scatter(part, "tp", scatter_dimension=0, tiled=True)

    rows = tok // 4
    (far,) = layer([lambda at: jnp.where(at < 2, 3, 0)], rows)
    inward, sides = [(0, 1), (3, 2)], [(0, 1), (1, 0), (2, 3), (3, 2)]
    got_far = lax.ppermute(far, "tp", inward)
    near, side, mine = layer(
        [lambda at: jnp.where(at < 2, 2, 1), lambda at: at ^ 1, lambda at: at], rows
    )
    halves = [near[: rows // 2], near[rows // 2 :]]
    got_near = [lax.ppermute(x, "tp", inward) for x in halves]
    got_side = lax.ppermute(side, "tp", sides)
    last = added(got_far, far)
    across = [lax.ppermute(last, "tp", [(1, 3), (2, 0)])]
    for got, x in zip(got_near, halves):
        last = added(after(got, last), x)
        across.append(lax.ppermute(last, "tp", [(1, 2), (2, 1)]))
    return added(mine, got_side, across[0], jnp.concatenate(across[1:], axis=0))


def solution(mesh):
    return jax.shard_map(
        body,
        mesh=mesh,
        in_specs=(P("seq", "tp"), P("seq", None), P("seq", None), P("tp", None)),
        out_specs=P(("seq", "tp"), None),
        check_vma=False,
    )
```

```python
import functools
import math

import jax
import jax.numpy as jnp
from jax import lax
from jax.experimental import pallas as pl
from jax.experimental.pallas import tpu as pltpu
from jax.sharding import PartitionSpec as P

QUERY_HEADS = 32
KEY_VALUE_HEADS = 8
HEAD_DIMENSION = 128
STRETCH = 8192
EXPONENT = HEAD_DIMENSION ** (-0.5) * math.log2(math.e)
NEGATIVE = -1e30
TILE = 512
GROUP = 6


def dot(a, b):
    return jnp.dot(a, b, preferred_element_type=jnp.float32)


def dot_nt(a, b):
    return lax.dot_general(a, b, (((1,), (1,)), ((), ())), preferred_element_type=jnp.float32)


def head(index):
    return slice(index * HEAD_DIMENSION, (index + 1) * HEAD_DIMENSION)


def spread(column):
    return jnp.broadcast_to(column, (column.shape[0], HEAD_DIMENSION))


def keys_of(blocks, g):
    return jnp.concatenate([block[:, head(g)] for block in blocks], axis=0)


def values_of(blocks, g, kv_here):
    values = keys_of(blocks, kv_here + g)
    return jnp.concatenate([values, jnp.ones_like(values)], axis=1)


def folded(query, keys, values, acc, top):
    score = dot_nt(query, keys)
    new = jnp.maximum(top, spread(jnp.max(score, axis=1, keepdims=True)))
    shrink = jnp.exp2((top - new) * EXPONENT)
    weight = jnp.exp2((score - new[:, :1]) * EXPONENT).astype(jnp.bfloat16)
    return acc * jnp.concatenate([shrink, shrink], axis=1) + dot(weight, values), new


def fetch(pairs, sems):
    copies = [pltpu.make_async_copy(src, dst, sems.at[i]) for i, (src, dst) in enumerate(pairs)]
    for copy in copies:
        copy.start()
    return copies


def pack_kernel(keys, values, own_ref, sems, *, per_kv, heads):
    half = own_ref.shape[1] // 2
    at = lax.axis_index("tp")
    if heads < per_kv:
        at = lax.div(at, per_kv // heads)
    cols = pl.ds(pl.multiple_of(at * half, HEAD_DIMENSION), half)
    for copy in fetch(
        [(keys.at[:, cols], own_ref.at[:, :half]), (values.at[:, cols], own_ref.at[:, half:])], sems
    ):
        copy.wait()


def stage_kernel(*refs):
    half = (len(refs) - 1) // 2
    for copy in fetch(list(zip(refs[:half], refs[half : 2 * half])), refs[-1]):
        copy.wait()


def layer_kernel(q_ref, *refs, heads, per_kv, chips, order, hops, first, last):
    chunks = len(order)
    count = 2 * first + len(hops)
    kv_ref, refs = refs[:count], refs[count:]
    if not first:
        acc_in, top_in, refs = refs[0], refs[1], refs[2:]
    if last:
        w_ref, outs, (acc_ref, top_ref, att_ref) = refs[0], refs[1 : 1 + chunks], refs[1 + chunks :]
    else:
        acc_ref, top_ref = refs
    rows = acc_ref.shape[2] // per_kv
    tok = kv_ref[0].shape[0]
    kv_here = heads // per_kv
    place = lax.rem(lax.axis_index("seq"), 2 * chips)
    chip, core = lax.div(place, 2), lax.rem(place, 2)
    tp_at = lax.axis_index("tp")
    starts = [pl.multiple_of(chunk(tp_at) * rows, rows) for chunk in order]
    there = [pl.ds(start, rows) for start in starts]
    here = [slice(i * rows, (i + 1) * rows) for i in range(chunks)]

    def every(step):
        for i in range(chunks):
            for g in range(kv_here):
                mine = range(g * per_kv, (g + 1) * per_kv)
                step(i, g, jnp.concatenate([q_ref[there[i], head(h)] for h in mine], axis=0))

    def own(i, g, query):
        score = dot_nt(query, keys_of(kv_ref[:2], g))
        row = lax.broadcasted_iota(jnp.int32, score.shape, 0) % rows + starts[i]
        col = lax.broadcasted_iota(jnp.int32, score.shape, 1)
        score = jnp.where(col <= jnp.where(col < tok, row, core * 2 * tok), score, NEGATIVE)
        top = jnp.max(score, axis=1, keepdims=True)
        weight = jnp.exp2((score - top) * EXPONENT).astype(jnp.bfloat16)
        acc_ref[i, g] = dot(weight, values_of(kv_ref[:2], g, kv_here))
        top_ref[i, g] = spread(top)

    def others(i, g, query, seen=None):
        acc_ref[i, g], top_ref[i, g] = folded(
            query, keys_of(seen, g), values_of(seen, g, kv_here), acc_ref[i, g], top_ref[i, g]
        )

    if first:
        every(own)
    else:
        acc_ref[...] = acc_in[...]
        top_ref[...] = top_in[...]
    blocks = kv_ref[2 * first :]
    bits = sorted({d.bit_length() - 1 for d in hops})
    some = {bit: [x for d, x in zip(hops, blocks) if d.bit_length() - 1 == bit] for bit in bits}
    seen = {bit: (chip >> bit) & 1 == 1 for bit in bits}

    def add(case, group):
        pl.when(case)(functools.partial(every, functools.partial(others, seen=group)))

    if len(hops) <= GROUP and len(bits) == 2:
        low, high = bits
        add(seen[low] & seen[high], some[high] + some[low])
        add(seen[low] & ~seen[high], some[low])
        add(~seen[low] & seen[high], some[high])
    else:
        for bit in bits:
            for at in range(0, len(some[bit]), GROUP):
                add(seen[bit], some[bit][at : at + GROUP])
    if not last:
        return
    for i in range(chunks):
        for h in range(heads):
            g, j = h // per_kv, h % per_kv
            state = acc_ref[i, g, j * rows : (j + 1) * rows, :]
            att_ref[here[i], head(h)] = (
                state[:, :HEAD_DIMENSION] / state[:, HEAD_DIMENSION:]
            ).astype(jnp.bfloat16)
    attended = att_ref[...]
    for at in range(0, w_ref.shape[1], TILE):
        part = dot(attended, w_ref[:, at : at + TILE]).astype(jnp.bfloat16)
        for i in range(chunks):
            outs[i][:, at : at + TILE] = part[here[i]]


def call(kernel, out_shape, *args, scratch, limit, place=pltpu.VMEM):
    return pl.pallas_call(
        kernel,
        out_shape=out_shape,
        in_specs=[pl.BlockSpec(memory_space=place)] * len(args),
        out_specs=[pl.BlockSpec(memory_space=pltpu.VMEM)] * len(out_shape),
        scratch_shapes=scratch,
        compiler_params=pltpu.CompilerParams(vmem_limit_bytes=limit * 2**20),
    )(*args)


def after(value, *others):
    return lax.optimization_barrier((value, *others))[0]


def added(*terms):
    total = terms[0].astype(jnp.float32)
    for term in terms[1:]:
        total = total + term.astype(jnp.float32)
    return total.astype(terms[0].dtype)


def body(queries, keys, values, out_weight):
    tok = queries.shape[0]
    hd = HEAD_DIMENSION
    heads = queries.shape[1] // hd
    group = QUERY_HEADS // KEY_VALUE_HEADS
    kv_here = max(1, heads // group)
    per_kv = heads // kv_here
    width = out_weight.shape[1]
    seq_devs, tp_devs = lax.axis_size("seq"), lax.axis_size("tp")
    pair_shape = (tok, 2 * kv_here * hd)
    semaphores = pltpu.SemaphoreType.DMA
    (own,) = call(
        functools.partial(pack_kernel, per_kv=group, heads=heads),
        [jax.ShapeDtypeStruct(pair_shape, keys.dtype)],
        keys,
        values,
        scratch=[semaphores((2,))],
        limit=56,
        place=pl.ANY,
    )
    devs = min(STRETCH // tok, seq_devs)
    chips = devs // 2

    swap = [(i, i ^ 1) for i in range(seq_devs)]
    blocks = [own]
    for d in range(1, chips):
        pairs = [(i, i ^ (2 * d)) for i in range(seq_devs) if i ^ (2 * d) > i]
        blocks.append(lax.ppermute(own, "seq", pairs))
    q_here, w_here = call(
        stage_kernel,
        [jax.ShapeDtypeStruct(x.shape, x.dtype) for x in (queries, out_weight)],
        queries,
        out_weight,
        scratch=[semaphores((2,))],
        limit=24,
        place=pl.ANY,
    )
    blocks[1:] = lax.optimization_barrier((*blocks[1:], q_here, w_here))[: chips - 1]
    swapped = [lax.ppermute(block, "seq", swap) for block in blocks]
    hops = list(range(1, chips))

    def layer(order, rows, seen, state=None, first=True, last=True):
        chunks = len(order)
        running = [(chunks, kv_here, per_kv * rows, 2 * hd), (chunks, kv_here, per_kv * rows, hd)]
        own_blocks = [own, swapped[0]] if first else []
        args = [*own_blocks, *[block for _, block in seen], *(state or []), *([w_here] * last)]
        return call(
            functools.partial(
                layer_kernel,
                heads=heads,
                per_kv=per_kv,
                chips=chips,
                order=order,
                hops=[d for d, _ in seen],
                first=first,
                last=last,
            ),
            [jax.ShapeDtypeStruct((rows, width), jnp.bfloat16)] * chunks
            if last
            else [jax.ShapeDtypeStruct(shape, jnp.float32) for shape in running],
            q_here,
            *args,
            scratch=[pltpu.VMEM(shape, jnp.float32) for shape in running]
            + [pltpu.VMEM((rows * chunks, heads * hd), jnp.bfloat16)]
            if last
            else [],
            limit=24,
        )

    got = list(zip(hops, blocks[1:]))
    theirs = list(zip(hops, swapped[1:]))
    if tp_devs != 4:
        (part,) = layer([lambda at: 0], tok, got + theirs)
        return lax.psum_scatter(part, "tp", scatter_dimension=0, tiled=True)

    rows = tok // 4
    far_rows = [lambda at: jnp.where(at < 2, 3, 0)]
    state = layer(far_rows, rows, got, last=False)
    (far,) = layer(far_rows, rows, theirs, state, first=False)
    inward, sides = [(0, 1), (3, 2)], [(0, 1), (1, 0), (2, 3), (3, 2)]
    got_far = lax.ppermute(far, "tp", inward)
    near, side, mine = layer(
        [lambda at: jnp.where(at < 2, 2, 1), lambda at: at ^ 1, lambda at: at], rows, got + theirs
    )
    half = rows // 2
    early, late = near[:half], near[half:]
    outward = [(1, 2), (2, 1)]
    got_direct = lax.ppermute(early, "tp", [(0, 2), (3, 1)])
    got_late = lax.ppermute(late, "tp", inward)
    got_side = lax.ppermute(side, "tp", sides)
    got_early = lax.ppermute(early, "tp", outward)
    total_far = added(got_far, far)
    across_far = lax.ppermute(total_far, "tp", [(1, 3), (2, 0)])
    got_late = after(got_late, got_direct, got_early, total_far)
    across_late = lax.ppermute(added(got_late, late), "tp", outward)
    return jnp.concatenate(
        [
            added(mine[:half], got_side[:half], across_far[:half], got_direct, got_early),
            added(mine[half:], got_side[half:], across_far[half:], across_late),
        ],
        axis=0,
    )


def solution(mesh):
    return jax.shard_map(
        body,
        mesh=mesh,
        in_specs=(P("seq", "tp"), P("seq", None), P("seq", None), P("tp", None)),
        out_specs=P(("seq", "tp"), None),
        check_vma=False,
    )
```

```python
import functools
import math

import jax
import jax.numpy as jnp
from jax import lax
from jax.experimental import pallas as pl
from jax.experimental.pallas import tpu as pltpu
from jax.sharding import PartitionSpec as P

QUERY_HEADS = 32
KEY_VALUE_HEADS = 8
HEAD_DIMENSION = 128
STRETCH = 8192
EXPONENT = HEAD_DIMENSION ** (-0.5) * math.log2(math.e)
NEGATIVE = -1e30
TILE = 512
GROUP = 6


def dot(a, b):
    return jnp.dot(a, b, preferred_element_type=jnp.float32)


def dot_nt(a, b):
    return lax.dot_general(a, b, (((1,), (1,)), ((), ())), preferred_element_type=jnp.float32)


def head(index):
    return slice(index * HEAD_DIMENSION, (index + 1) * HEAD_DIMENSION)


def spread(column):
    return jnp.broadcast_to(column, (column.shape[0], HEAD_DIMENSION))


def keys_of(blocks, g):
    return jnp.concatenate([block[:, head(g)] for block in blocks], axis=0)


def values_of(blocks, g, kv_here):
    values = keys_of(blocks, kv_here + g)
    return jnp.concatenate([values, jnp.ones_like(values)], axis=1)


def folded(query, keys, values, acc, top):
    score = dot_nt(query, keys)
    new = jnp.maximum(top, spread(jnp.max(score, axis=1, keepdims=True)))
    shrink = jnp.exp2((top - new) * EXPONENT)
    weight = jnp.exp2((score - new[:, :1]) * EXPONENT).astype(jnp.bfloat16)
    return acc * jnp.concatenate([shrink, shrink], axis=1) + dot(weight, values), new


def fetch(pairs, sems):
    copies = [pltpu.make_async_copy(src, dst, sems.at[i]) for i, (src, dst) in enumerate(pairs)]
    for copy in copies:
        copy.start()
    return copies


def pack_kernel(keys, values, own_ref, sems, *, per_kv, heads):
    half = own_ref.shape[1] // 2
    at = lax.axis_index("tp")
    if heads < per_kv:
        at = lax.div(at, per_kv // heads)
    cols = pl.ds(pl.multiple_of(at * half, HEAD_DIMENSION), half)
    for copy in fetch(
        [(keys.at[:, cols], own_ref.at[:, :half]), (values.at[:, cols], own_ref.at[:, half:])], sems
    ):
        copy.wait()


def stage_kernel(*refs):
    half = (len(refs) - 1) // 2
    for copy in fetch(list(zip(refs[:half], refs[half : 2 * half])), refs[-1]):
        copy.wait()


def layer_kernel(q_ref, *refs, heads, per_kv, chips, order, outer, hops, first, last):
    chunks = len(order)
    count = 2 * first + len(hops)
    kv_ref, refs = refs[:count], refs[count:]
    if not first:
        acc_in, top_in, refs = refs[0], refs[1], refs[2:]
    if last:
        w_ref, outs, (acc_ref, top_ref, att_ref) = refs[0], refs[1 : 1 + chunks], refs[1 + chunks :]
    else:
        acc_ref, top_ref = refs
    rows = acc_ref.shape[2] // per_kv
    tok = kv_ref[0].shape[0]
    kv_here = heads // per_kv
    place = lax.rem(lax.axis_index("seq"), 2 * chips)
    chip, core = lax.div(place, 2), lax.rem(place, 2)
    tp_at = lax.axis_index("tp")
    starts = [pl.multiple_of(chunk(tp_at) * rows, rows) for chunk in order]
    there = [pl.ds(start, rows) for start in starts]
    here = [slice(i * rows, (i + 1) * rows) for i in range(chunks)]

    def run(begin):
        attend(range(begin, chunks))
        if last:
            project(range(begin, chunks))

    def every(step, todo):
        for i in todo:
            for g in range(kv_here):
                mine = range(g * per_kv, (g + 1) * per_kv)
                step(i, g, jnp.concatenate([q_ref[there[i], head(h)] for h in mine], axis=0))

    def own(i, g, query):
        score = dot_nt(query, keys_of(kv_ref[:2], g))
        row = lax.broadcasted_iota(jnp.int32, score.shape, 0) % rows + starts[i]
        col = lax.broadcasted_iota(jnp.int32, score.shape, 1)
        score = jnp.where(col <= jnp.where(col < tok, row, core * 2 * tok), score, NEGATIVE)
        top = jnp.max(score, axis=1, keepdims=True)
        weight = jnp.exp2((score - top) * EXPONENT).astype(jnp.bfloat16)
        acc_ref[i, g] = dot(weight, values_of(kv_ref[:2], g, kv_here))
        top_ref[i, g] = spread(top)

    def others(i, g, query, seen=None):
        acc_ref[i, g], top_ref[i, g] = folded(
            query, keys_of(seen, g), values_of(seen, g, kv_here), acc_ref[i, g], top_ref[i, g]
        )

    blocks = kv_ref[2 * first :]
    bits = sorted({d.bit_length() - 1 for d in hops})
    some = {bit: [x for d, x in zip(hops, blocks) if d.bit_length() - 1 == bit] for bit in bits}
    seen = {bit: (chip >> bit) & 1 == 1 for bit in bits}

    def attend(todo):
        if first:
            every(own, todo)
        else:
            acc_ref[...] = acc_in[...]
            top_ref[...] = top_in[...]

        def add(case, group):
            step = functools.partial(others, seen=group)
            pl.when(case)(functools.partial(every, step, todo))

        if len(hops) <= GROUP and len(bits) == 2:
            low, high = bits
            add(seen[low] & seen[high], some[high] + some[low])
            add(seen[low] & ~seen[high], some[low])
            add(~seen[low] & seen[high], some[high])
        else:
            for bit in bits:
                for at in range(0, len(some[bit]), GROUP):
                    add(seen[bit], some[bit][at : at + GROUP])

    def project(todo):
        for i in todo:
            for h in range(heads):
                g, j = h // per_kv, h % per_kv
                state = acc_ref[i, g, j * rows : (j + 1) * rows, :]
                att_ref[here[i], head(h)] = (
                    state[:, :HEAD_DIMENSION] / state[:, HEAD_DIMENSION:]
                ).astype(jnp.bfloat16)
        attended = att_ref[todo[0] * rows :, :]
        for at in range(0, w_ref.shape[1], TILE):
            part = dot(attended, w_ref[:, at : at + TILE]).astype(jnp.bfloat16)
            for j, i in enumerate(todo):
                outs[i][:, at : at + TILE] = part[here[j]]

    if len(set(outer)) == 1:
        run(outer[0])
        return
    is_outer = (tp_at == 0) | (tp_at == 3)
    for case, begin in ((is_outer, outer[0]), (~is_outer, outer[1])):
        if begin < chunks:
            pl.when(case)(functools.partial(run, begin))
        for out in outs[:begin] if last else []:

            @pl.when(case)
            def _(out=out):
                out[...] = jnp.zeros_like(out)


def add_kernel(*refs, half):
    *terms, out = refs
    mine, side, far, direct, early, late = terms
    for rows, more in ((slice(0, half), [direct, early]), (slice(half, 2 * half), [late])):
        total = mine[rows].astype(jnp.float32) + side[rows].astype(jnp.float32)
        total = total + far[rows].astype(jnp.float32)
        for term in more:
            total = total + term[...].astype(jnp.float32)
        out[rows] = total.astype(out.dtype)


def call(kernel, out_shape, *args, scratch, limit, place=pltpu.VMEM):
    return pl.pallas_call(
        kernel,
        out_shape=out_shape,
        in_specs=[pl.BlockSpec(memory_space=place)] * len(args),
        out_specs=[pl.BlockSpec(memory_space=pltpu.VMEM)] * len(out_shape),
        scratch_shapes=scratch,
        compiler_params=pltpu.CompilerParams(vmem_limit_bytes=limit * 2**20),
    )(*args)


def after(value, *others):
    return lax.optimization_barrier((value, *others))[0]


def added(*terms):
    total = terms[0].astype(jnp.float32)
    for term in terms[1:]:
        total = total + term.astype(jnp.float32)
    return total.astype(terms[0].dtype)


def body(queries, keys, values, out_weight):
    tok = queries.shape[0]
    hd = HEAD_DIMENSION
    heads = queries.shape[1] // hd
    group = QUERY_HEADS // KEY_VALUE_HEADS
    kv_here = max(1, heads // group)
    per_kv = heads // kv_here
    width = out_weight.shape[1]
    seq_devs, tp_devs = lax.axis_size("seq"), lax.axis_size("tp")
    pair_shape = (tok, 2 * kv_here * hd)
    semaphores = pltpu.SemaphoreType.DMA
    (own,) = call(
        functools.partial(pack_kernel, per_kv=group, heads=heads),
        [jax.ShapeDtypeStruct(pair_shape, keys.dtype)],
        keys,
        values,
        scratch=[semaphores((2,))],
        limit=56,
        place=pl.ANY,
    )
    devs = min(STRETCH // tok, seq_devs)
    chips = devs // 2

    swap = [(i, i ^ 1) for i in range(seq_devs)]
    blocks = [own]
    for d in range(1, chips):
        pairs = [(i, i ^ (2 * d)) for i in range(seq_devs) if i ^ (2 * d) > i]
        blocks.append(lax.ppermute(own, "seq", pairs))
    q_here, w_here = call(
        stage_kernel,
        [jax.ShapeDtypeStruct(x.shape, x.dtype) for x in (queries, out_weight)],
        queries,
        out_weight,
        scratch=[semaphores((2,))],
        limit=24,
        place=pl.ANY,
    )
    blocks[1:] = lax.optimization_barrier((*blocks[1:], q_here, w_here))[: chips - 1]
    swapped = [lax.ppermute(block, "seq", swap) for block in blocks]
    hops = list(range(1, chips))

    def layer(order, rows, seen, state=None, first=True, last=True, outer=(0, 0)):
        chunks = len(order)
        running = [(chunks, kv_here, per_kv * rows, 2 * hd), (chunks, kv_here, per_kv * rows, hd)]
        own_blocks = [own, swapped[0]] if first else []
        args = [*own_blocks, *[block for _, block in seen], *(state or []), *([w_here] * last)]
        return call(
            functools.partial(
                layer_kernel,
                heads=heads,
                per_kv=per_kv,
                chips=chips,
                order=order,
                outer=outer,
                hops=[d for d, _ in seen],
                first=first,
                last=last,
            ),
            [jax.ShapeDtypeStruct((rows, width), jnp.bfloat16)] * chunks
            if last
            else [jax.ShapeDtypeStruct(shape, jnp.float32) for shape in running],
            q_here,
            *args,
            scratch=[pltpu.VMEM(shape, jnp.float32) for shape in running]
            + [pltpu.VMEM((rows * chunks, heads * hd), jnp.bfloat16)]
            if last
            else [],
            limit=24,
        )

    got = list(zip(hops, blocks[1:]))
    theirs = list(zip(hops, swapped[1:]))
    if tp_devs != 4:
        (part,) = layer([lambda at: 0], tok, got + theirs)
        return lax.psum_scatter(part, "tp", scatter_dimension=0, tiled=True)

    rows = tok // 4
    far_rows = [lambda at: jnp.where(at < 2, 3, 0)]
    state = layer(far_rows, rows, got, last=False, outer=(0, 1))
    (far,) = layer(far_rows, rows, theirs, state, first=False, outer=(0, 1))
    inward, sides = [(0, 1), (3, 2)], [(0, 1), (1, 0), (2, 3), (3, 2)]
    got_far = lax.ppermute(far, "tp", inward)
    far_here, near, side, mine = layer(
        far_rows + [lambda at: jnp.where(at < 2, 2, 1), lambda at: at ^ 1, lambda at: at],
        rows,
        got + theirs,
        outer=(1, 0),
    )
    half = rows // 2
    early, late = near[:half], near[half:]
    outward = [(1, 2), (2, 1)]
    got_direct = lax.ppermute(early, "tp", [(0, 2), (3, 1)])
    got_late = lax.ppermute(late, "tp", inward)
    got_side = lax.ppermute(side, "tp", sides)
    got_early = lax.ppermute(early, "tp", outward)
    total_far = added(got_far, far_here)
    across_far = lax.ppermute(total_far, "tp", [(1, 3), (2, 0)])
    got_late = after(got_late, got_direct, got_early, total_far)
    across_late = lax.ppermute(added(got_late, late), "tp", outward)
    (out,) = call(
        functools.partial(add_kernel, half=half),
        [jax.ShapeDtypeStruct(mine.shape, mine.dtype)],
        mine,
        got_side,
        across_far,
        got_direct,
        got_early,
        across_late,
        scratch=[],
        limit=24,
    )
    return out


def solution(mesh):
    return jax.shard_map(
        body,
        mesh=mesh,
        in_specs=(P("seq", "tp"), P("seq", None), P("seq", None), P("tp", None)),
        out_specs=P(("seq", "tp"), None),
        check_vma=False,
    )
```

```python
import functools
import math

import jax
import jax.numpy as jnp
from jax import lax
from jax.experimental import pallas as pl
from jax.experimental.pallas import tpu as pltpu
from jax.sharding import PartitionSpec as P

QUERY_HEADS = 32
KEY_VALUE_HEADS = 8
HEAD_DIMENSION = 128
STRETCH = 8192
EXPONENT = HEAD_DIMENSION ** (-0.5) * math.log2(math.e)
NEGATIVE = -1e30
TILE = 512
GROUP = 6
ROWS = 16


def dot(a, b):
    return jnp.dot(a, b, preferred_element_type=jnp.float32)


def dot_nt(a, b):
    return lax.dot_general(a, b, (((1,), (1,)), ((), ())), preferred_element_type=jnp.float32)


def head(index):
    return slice(index * HEAD_DIMENSION, (index + 1) * HEAD_DIMENSION)


def spread(column):
    return jnp.broadcast_to(column, (column.shape[0], HEAD_DIMENSION))


def keys_of(blocks, g):
    return jnp.concatenate([block[:, head(g)] for block in blocks], axis=0)


def values_of(blocks, g, kv_here):
    values = keys_of(blocks, kv_here + g)
    return jnp.concatenate([values, jnp.ones_like(values)], axis=1)


def folded(query, keys, values, acc, top):
    score = dot_nt(query, keys)
    new = jnp.maximum(top, spread(jnp.max(score, axis=1, keepdims=True)))
    shrink = jnp.exp2((top - new) * EXPONENT)
    weight = jnp.exp2((score - new[:, :1]) * EXPONENT).astype(jnp.bfloat16)
    return acc * jnp.concatenate([shrink, shrink], axis=1) + dot(weight, values), new


def fetch(pairs, sems):
    copies = [pltpu.make_async_copy(src, dst, sems.at[i]) for i, (src, dst) in enumerate(pairs)]
    for copy in copies:
        copy.start()
    return copies


def pack_kernel(keys, values, own_ref, sems, *, per_kv, heads):
    half = own_ref.shape[1] // 2
    at = lax.axis_index("tp")
    if heads < per_kv:
        at = lax.div(at, per_kv // heads)
    cols = pl.ds(pl.multiple_of(at * half, HEAD_DIMENSION), half)
    for copy in fetch(
        [(keys.at[:, cols], own_ref.at[:, :half]), (values.at[:, cols], own_ref.at[:, half:])], sems
    ):
        copy.wait()


def stage_kernel(*refs):
    half = (len(refs) - 1) // 2
    for copy in fetch(list(zip(refs[:half], refs[half : 2 * half])), refs[-1]):
        copy.wait()


def layer_kernel(q_ref, *refs, heads, per_kv, chips, order, outer, hops, first, last, split=None, upto=None):
    chunks = len(order)
    count = 2 * first + len(hops)
    kv_ref, refs = refs[:count], refs[count:]
    if not first:
        acc_in, top_in, refs = refs[0], refs[1], refs[2:]
    if last:
        w_ref, outs, (acc_ref, top_ref, att_ref) = refs[0], list(refs[1:-3]), refs[-3:]
        if upto:
            outs, att_ref, acc_ref, top_ref = outs[:-1], outs[-1], *refs[-3:-1]
        if split:
            chunk, column = split
            outs[chunk : chunk + 2] = [(outs[chunk], outs[chunk + 1])]
    else:
        acc_ref, top_ref = refs
    rows = acc_ref.shape[2] // per_kv
    tok = kv_ref[0].shape[0]
    kv_here = heads // per_kv
    place = lax.rem(lax.axis_index("seq"), 2 * chips)
    chip, core = lax.div(place, 2), lax.rem(place, 2)
    tp_at = lax.axis_index("tp")
    starts = [pl.multiple_of(chunk(tp_at) * rows, rows) for chunk in order]
    there = [pl.ds(start, rows) for start in starts]
    here = [slice(i * rows, (i + 1) * rows) for i in range(chunks)]

    def run(begin):
        attend(range(begin, chunks))
        if last:
            project(range(begin, chunks))

    def every(step, todo):
        for i in todo:
            for g in range(kv_here):
                mine = range(g * per_kv, (g + 1) * per_kv)
                step(i, g, jnp.concatenate([q_ref[there[i], head(h)] for h in mine], axis=0))

    def own(i, g, query):
        score = dot_nt(query, keys_of(kv_ref[:2], g))
        row = lax.broadcasted_iota(jnp.int32, score.shape, 0) % rows + starts[i]
        col = lax.broadcasted_iota(jnp.int32, score.shape, 1)
        score = jnp.where(col <= jnp.where(col < tok, row, core * 2 * tok), score, NEGATIVE)
        top = jnp.max(score, axis=1, keepdims=True)
        weight = jnp.exp2((score - top) * EXPONENT).astype(jnp.bfloat16)
        acc_ref[i, g] = dot(weight, values_of(kv_ref[:2], g, kv_here))
        top_ref[i, g] = spread(top)

    def others(i, g, query, seen=None):
        acc_ref[i, g], top_ref[i, g] = folded(
            query, keys_of(seen, g), values_of(seen, g, kv_here), acc_ref[i, g], top_ref[i, g]
        )

    blocks = kv_ref[2 * first :]
    bits = sorted({d.bit_length() - 1 for d in hops})
    some = {bit: [x for d, x in zip(hops, blocks) if d.bit_length() - 1 == bit] for bit in bits}
    seen = {bit: (chip >> bit) & 1 == 1 for bit in bits}

    def attend(todo):
        if first:
            every(own, todo)
        else:
            acc_ref[...] = acc_in[...]
            top_ref[...] = top_in[...]

        def add(case, group):
            step = functools.partial(others, seen=group)
            pl.when(case)(functools.partial(every, step, todo))

        if len(hops) <= GROUP and len(bits) == 2:
            low, high = bits
            add(seen[low] & seen[high], some[high] + some[low])
            add(seen[low] & ~seen[high], some[low])
            add(~seen[low] & seen[high], some[high])
        else:
            for bit in bits:
                for at in range(0, len(some[bit]), GROUP):
                    add(seen[bit], some[bit][at : at + GROUP])

    def project(todo):
        for i in todo:
            for h in range(heads):
                g, j = h // per_kv, h % per_kv
                state = acc_ref[i, g, j * rows : (j + 1) * rows, :]
                att_ref[here[i], head(h)] = (
                    state[:, :HEAD_DIMENSION] / state[:, HEAD_DIMENSION:]
                ).astype(jnp.bfloat16)
        attended = att_ref[todo[0] * rows :, :]
        for at in range(0, upto or w_ref.shape[1], TILE):
            part = dot(attended, w_ref[:, at : at + TILE]).astype(jnp.bfloat16)
            for j, i in enumerate(todo):
                out, to = outs[i], at
                if isinstance(out, tuple):
                    out, to = (out[0], at) if at < column else (out[1], at - column)
                out[:, to : to + TILE] = part[here[j]]

    if len(set(outer)) == 1:
        run(outer[0])
        return
    is_outer = (tp_at == 0) | (tp_at == 3)
    for case, begin in ((is_outer, outer[0]), (~is_outer, outer[1])):
        if begin < chunks:
            pl.when(case)(functools.partial(run, begin))
        for out in outs[:begin] if last else []:

            @pl.when(case)
            def _(out=out):
                out[...] = jnp.zeros_like(out)


def project_kernel(att_ref, w_ref, out, *, begin):
    tp_at = lax.axis_index("tp")
    is_outer = (tp_at == 0) | (tp_at == 3)

    @pl.when(is_outer)
    def _():
        attended = att_ref[...]
        for at in range(begin, w_ref.shape[1], TILE):
            part = dot(attended, w_ref[:, at : at + TILE])
            out[:, at - begin : at - begin + TILE] = part.astype(jnp.bfloat16)

    @pl.when(~is_outer)
    def _():
        out[...] = jnp.zeros_like(out)


def add_kernel(mine, side, far, direct, early, late, out, sum_ref, sems):
    column = direct.shape[1]
    copies = []
    for i, at in enumerate(range(0, out.shape[0], ROWS)):
        rows = slice(at, at + ROWS)
        for cols, more in ((slice(0, column), [direct, early]), (slice(column, None), [late])):
            total = mine[rows, cols].astype(jnp.float32) + side[rows, cols].astype(jnp.float32)
            total = total + far[rows, cols].astype(jnp.float32)
            for term in more:
                total = total + term[rows].astype(jnp.float32)
            sum_ref[rows, cols] = total.astype(out.dtype)
        copies.append(pltpu.make_async_copy(sum_ref.at[rows], out.at[rows], sems.at[i]))
        copies[-1].start()
    for copy in copies:
        copy.wait()


def call(kernel, out_shape, *args, scratch, limit, place=pltpu.VMEM, result=pltpu.VMEM):
    return pl.pallas_call(
        kernel,
        out_shape=out_shape,
        in_specs=[pl.BlockSpec(memory_space=place)] * len(args),
        out_specs=[pl.BlockSpec(memory_space=result)] * len(out_shape),
        scratch_shapes=scratch,
        compiler_params=pltpu.CompilerParams(vmem_limit_bytes=limit * 2**20),
    )(*args)


def after(value, *others):
    return lax.optimization_barrier((value, *others))[0]


def added(*terms):
    total = terms[0].astype(jnp.float32)
    for term in terms[1:]:
        total = total + term.astype(jnp.float32)
    return total.astype(terms[0].dtype)


def body(queries, keys, values, out_weight):
    tok = queries.shape[0]
    hd = HEAD_DIMENSION
    heads = queries.shape[1] // hd
    group = QUERY_HEADS // KEY_VALUE_HEADS
    kv_here = max(1, heads // group)
    per_kv = heads // kv_here
    width = out_weight.shape[1]
    seq_devs, tp_devs = lax.axis_size("seq"), lax.axis_size("tp")
    pair_shape = (tok, 2 * kv_here * hd)
    semaphores = pltpu.SemaphoreType.DMA
    (own,) = call(
        functools.partial(pack_kernel, per_kv=group, heads=heads),
        [jax.ShapeDtypeStruct(pair_shape, keys.dtype)],
        keys,
        values,
        scratch=[semaphores((2,))],
        limit=56,
        place=pl.ANY,
    )
    devs = min(STRETCH // tok, seq_devs)
    chips = devs // 2

    swap = [(i, i ^ 1) for i in range(seq_devs)]
    blocks = [own]
    for d in range(1, chips):
        pairs = [(i, i ^ (2 * d)) for i in range(seq_devs) if i ^ (2 * d) > i]
        blocks.append(lax.ppermute(own, "seq", pairs))
    q_here, w_here = call(
        stage_kernel,
        [jax.ShapeDtypeStruct(x.shape, x.dtype) for x in (queries, out_weight)],
        queries,
        out_weight,
        scratch=[semaphores((2,))],
        limit=24,
        place=pl.ANY,
    )
    blocks[1:] = [after(block, q_here, w_here) for block in blocks[1:]]
    swapped = [lax.ppermute(block, "seq", swap) for block in blocks]
    slow = chips // 2
    swapped[slow] = lax.ppermute(after(blocks[slow], *swapped[1:slow], *swapped[slow + 1 :]), "seq", swap)
    hops = list(range(1, chips))

    def layer(order, rows, seen, state=None, first=True, last=True, outer=(0, 0), split=None, upto=None):
        chunks = len(order)
        running = [(chunks, kv_here, per_kv * rows, 2 * hd), (chunks, kv_here, per_kv * rows, hd)]
        widths = [width] * chunks
        if split:
            widths[split[0] : split[0] + 1] = [split[1], width - split[1]]
        if upto:
            widths = [upto]
        own_blocks = [own, swapped[0]] if first else []
        args = [*own_blocks, *[block for _, block in seen], *(state or []), *([w_here] * last)]
        return call(
            functools.partial(
                layer_kernel,
                heads=heads,
                per_kv=per_kv,
                chips=chips,
                order=order,
                outer=outer,
                hops=[d for d, _ in seen],
                first=first,
                last=last,
                split=split,
                upto=upto,
            ),
            [jax.ShapeDtypeStruct((rows, columns), jnp.bfloat16) for columns in widths]
            + ([jax.ShapeDtypeStruct((rows * chunks, heads * hd), jnp.bfloat16)] if upto else [])
            if last
            else [jax.ShapeDtypeStruct(shape, jnp.float32) for shape in running],
            q_here,
            *args,
            scratch=[pltpu.VMEM(shape, jnp.float32) for shape in running]
            + [pltpu.VMEM((rows * chunks, heads * hd), jnp.bfloat16)]
            if last
            else [],
            limit=24,
        )

    got = list(zip(hops, blocks[1:]))
    theirs = list(zip(hops, swapped[1:]))
    if tp_devs != 4:
        (part,) = layer([lambda at: 0], tok, got + theirs)
        return lax.psum_scatter(part, "tp", scatter_dimension=0, tiled=True)

    rows = tok // 4
    far_rows = [lambda at: jnp.where(at < 2, 3, 0)]
    soon = [(d, block) for d, block in theirs if d != slow]
    then = [(d, block) for d, block in theirs if d == slow]
    state = layer(far_rows, rows, got + soon, last=False, outer=(0, 1))
    begin = width * 3 // 5 // TILE * TILE
    far, attended = layer(far_rows, rows, then, state, first=False, outer=(0, 1), upto=begin)
    inward, sides = [(0, 1), (3, 2)], [(0, 1), (1, 0), (2, 3), (3, 2)]
    got_far = [lax.ppermute(far, "tp", inward)]
    (far_rest,) = call(
        functools.partial(project_kernel, begin=begin),
        [jax.ShapeDtypeStruct((rows, width - begin), jnp.bfloat16)],
        attended,
        w_here,
        scratch=[],
        limit=24,
    )
    got_far.append(lax.ppermute(far_rest, "tp", inward))
    column = width * 2 // 5 // TILE * TILE
    far_here, early, late, side, mine = layer(
        far_rows + [lambda at: jnp.where(at < 2, 2, 1), lambda at: at ^ 1, lambda at: at],
        rows,
        got + theirs,
        outer=(1, 0),
        split=(1, column),
    )
    outward = [(1, 2), (2, 1)]
    got_direct = lax.ppermute(early, "tp", [(0, 2), (3, 1)])
    got_late = lax.ppermute(late, "tp", inward)
    got_side = lax.ppermute(side, "tp", sides)
    got_early = lax.ppermute(early, "tp", outward)
    total_far = added(jnp.concatenate(got_far, axis=1), far_here)
    across_far = lax.ppermute(total_far, "tp", [(1, 3), (2, 0)])
    got_late = after(got_late, got_direct, got_early, total_far)
    across_late = lax.ppermute(added(got_late, late), "tp", outward)
    (out,) = call(
        add_kernel,
        [jax.ShapeDtypeStruct(mine.shape, mine.dtype)],
        mine,
        got_side,
        across_far,
        got_direct,
        got_early,
        across_late,
        scratch=[
            pltpu.VMEM(mine.shape, mine.dtype),
            semaphores((rows // ROWS,)),
        ],
        limit=24,
        result=pl.ANY,
    )
    return out


def solution(mesh):
    return jax.shard_map(
        body,
        mesh=mesh,
        in_specs=(P("seq", "tp"), P("seq", None), P("seq", None), P("tp", None)),
        out_specs=P(("seq", "tp"), None),
        check_vma=False,
    )
```
